32 devices in a mesh: view: 2 (over y), seq: 16 (over z, x, core).
Axes of the slice: x: 2, y: 2, z: 4, core: 2. Of those that a mesh axis runs over, the one named last changes fastest.
Arguments:
- queries: bfloat16 [4, 2, 2048, 2048], P(None, 'view', 'seq'), may hold values from -6 to 6
- key_rows: bfloat16 [4, 2, 2048, 2048], P(None, 'view', 'seq'), may hold values from -6 to 6
- value_rows: bfloat16 [4, 2, 2048, 2048], P(None, 'view', 'seq'), may hold values from -6 to 6
- view_queries: bfloat16 [4, 2, 2048, 2048], P(None, 'view', 'seq'), may hold values from -6 to 6
Outputs:
- spatial: bfloat16 [4, 2, 2048, 2048], P(None, 'view', 'seq')
- joined: bfloat16 [4, 2, 2048, 2048], P(None, 'view', 'seq')
The draws below stay inside these ranges and needn't reach their ends.
All inputs are finite; a program needn't handle non-finite values.
Results may differ from the reference program's by a relative error of at most 0.0064.
Values may be sent and summed in bfloat16 or wider, within the bound.
No kernel may reach another device: no remote copies, remote signals or barrier semaphores. Data moves between devices by JAX's collectives and lax.ppermute only.
A program may use at most 128 MiB of HBM per device.

```python
import jax
import jax.numpy as jnp
from jax import lax

HEADS = 32
HEAD_DIM = 64
D = 2048
BATCH = 4
SEQ_LEN = 2048
VIEWS = 2


def draw_queries(key, part):
    key = jax.random.fold_in(key, 1)
    full_shape = (BATCH, VIEWS, SEQ_LEN, HEADS, HEAD_DIM)
    noise = jnp.clip(jax.random.normal(key, full_shape, jnp.float32), -6.0, 6.0)
    return noise.reshape(BATCH, VIEWS, SEQ_LEN, HEADS * HEAD_DIM).astype(jnp.bfloat16)


def draw_key_rows(key, part):
    key = jax.random.fold_in(key, 2)
    full_shape = (BATCH, VIEWS, SEQ_LEN, HEADS, HEAD_DIM)
    noise = jnp.clip(jax.random.normal(key, full_shape, jnp.float32), -6.0, 6.0)
    return noise.reshape(BATCH, VIEWS, SEQ_LEN, HEADS * HEAD_DIM).astype(jnp.bfloat16)


def draw_view_queries(key, part):
    key = jax.random.fold_in(key, 3)
    full_shape = (BATCH, VIEWS, SEQ_LEN, HEADS, HEAD_DIM)
    noise = jnp.clip(jax.random.normal(key, full_shape, jnp.float32), -6.0, 6.0)
    return noise.reshape(BATCH, VIEWS, SEQ_LEN, HEADS * HEAD_DIM).astype(jnp.bfloat16)


def block_levels(stream_key, extent, shards, smallest, largest):
    loudness, own = 1.0, jax.random.fold_in(stream_key, 6)
    for axis_at, parts in shards:
        steps = jnp.exp(jax.random.uniform(jax.random.fold_in(own, axis_at), (parts,), jnp.float32, smallest / len(shards), largest / len(shards)))
        loudness = loudness * jnp.repeat(steps, extent[axis_at] // parts).reshape([-1 if axis == axis_at else 1 for axis in range(len(extent))])
    return loudness


def bell_draw(rng, extent, spread, bound, cuts=(), kind=jnp.bfloat16):
    level = block_levels(rng, extent, cuts, -0.22, 0.18) if cuts else 1.0
    entries = jax.random.normal(rng, extent, jnp.float32) * spread * level
    return jnp.minimum(jnp.maximum(entries, -bound), bound).astype(kind)


def setup_inputs(seed: int = 0) -> dict:
    key_list = jax.random.split(jax.random.key(seed), 5)
    return {
        "queries": draw_queries(jax.random.fold_in(key_list[4], 71), 0),
        "key_rows": draw_key_rows(jax.random.fold_in(key_list[4], 71), 0),
        "value_rows": bell_draw(key_list[2], (BATCH, VIEWS, SEQ_LEN, D), 1.0, 6.0, ((1, 2), (2, 16))),
        "view_queries": draw_view_queries(jax.random.fold_in(key_list[4], 71), 0),
    }


def view_attention(triple):
    query_part, key_part, value_part = triple
    length = query_part.shape[0]
    block_rows = min(512, length)
    score_scale = HEAD_DIM ** -0.5
    key_full = key_part.astype(jnp.float32)
    value_full = value_part.astype(jnp.float32)

    def one_block(query_block):
        scores = jnp.einsum("qhe,khe->hqk", query_block.astype(jnp.float32), key_full) * score_scale
        scores = scores - jnp.max(scores, axis=-1, keepdims=True)
        expo = jnp.exp(scores)
        weights = (expo / jnp.sum(expo, axis=-1, keepdims=True)).astype(jnp.bfloat16)
        weights = lax.optimization_barrier(weights).astype(jnp.float32)
        result = jnp.einsum("hqk,khe->qhe", weights, value_full)
        return result.astype(jnp.bfloat16)

    blocks = query_part.reshape(length // block_rows, block_rows, HEADS, HEAD_DIM)
    return lax.map(one_block, blocks).reshape(length, HEADS, HEAD_DIM)


def across_views(triple):
    cross_query, key_part, output_part = triple
    score_scale = HEAD_DIM ** -0.5
    scores = jnp.einsum("vshe,wshe->shvw", cross_query.astype(jnp.float32), key_part.astype(jnp.float32)) * score_scale
    scores = scores - jnp.max(scores, axis=-1, keepdims=True)
    expo = jnp.exp(scores)
    weights = (expo / jnp.sum(expo, axis=-1, keepdims=True)).astype(jnp.bfloat16)
    weights = lax.optimization_barrier(weights).astype(jnp.float32)
    result = jnp.einsum("shvw,wshe->vshe", weights, output_part.astype(jnp.float32))
    return result.astype(jnp.bfloat16)


def reference(queries, key_rows, value_rows, view_queries):
    batch_size, view_count, length, model_width = queries.shape
    flat_shape = (batch_size * view_count, length, HEADS, HEAD_DIM)
    spatial = lax.map(view_attention, (queries.reshape(flat_shape), key_rows.reshape(flat_shape), value_rows.reshape(flat_shape)))
    spatial = spatial.reshape(batch_size, view_count, length, model_width)
    split_shape = (batch_size, view_count, length, HEADS, HEAD_DIM)
    joined = lax.map(across_views, (view_queries.reshape(split_shape), key_rows.reshape(split_shape), spatial.reshape(split_shape)))
    joined = joined.reshape(batch_size, view_count, length, model_width)
    return spatial, joined
```

```python
import functools
import math

import jax
import jax.numpy as jnp
from jax import lax
from jax.experimental import pallas as pl
from jax.experimental.pallas import tpu as pltpu
from jax.sharding import PartitionSpec as P

HEADS = 32
LANES = 128
VMEM_LIMIT = 48 * 1024 * 1024


def block_place(me, shift, lane_blocks, per_chunk):
    other = me ^ shift
    video = 0 if per_chunk == 1 else other // lane_blocks
    column = other if per_chunk == 1 else other % lane_blocks
    return video, pl.ds(pl.multiple_of(column * LANES, LANES), LANES)


def source_copies(me, first_batch, per_chunk, sources, targets, sems):
    rows = sources[0].shape[2]
    lane_blocks = sources[0].shape[3] // LANES
    copies = []
    for shift, target in enumerate(targets):
        video, lanes = block_place(me, shift, lane_blocks, per_chunk)
        for which, source in enumerate(sources):
            copies.append(
                pltpu.make_async_copy(
                    source.at[first_batch + video, 0, :, lanes],
                    target.at[pl.ds(which * rows, rows), :],
                    sems.at[len(copies)],
                )
            )
    return copies


def pack_kernel(first_batch, per_chunk, me_ref, q_ref, k_ref, v_ref, *refs):
    targets, sems = refs[:-1], refs[-1]
    copies = source_copies(
        me_ref[0], first_batch, per_chunk, (q_ref, k_ref, v_ref), targets, sems
    )
    for copy in copies:
        copy.start()
    for copy in copies:
        copy.wait()


def pack(me, sources, first_batch, per_chunk, parts):
    rows = sources[0].shape[2]
    dtype = sources[0].dtype
    anywhere = pl.BlockSpec(memory_space=pl.ANY)
    return pl.pallas_call(
        functools.partial(pack_kernel, first_batch, per_chunk),
        in_specs=[pl.BlockSpec(memory_space=pltpu.SMEM)] + [anywhere] * 3,
        out_specs=[anywhere] * parts,
        out_shape=[jax.ShapeDtypeStruct((3 * rows, LANES), dtype)] * parts,
        scratch_shapes=[pltpu.SemaphoreType.DMA((3 * parts,))],
        cost_estimate=pl.CostEstimate(
            flops=0, bytes_accessed=parts * 3 * rows * LANES * 4, transcendentals=0
        ),
        name="pack",
    )(me, *sources)


def attend_kernel(parts, rows, group, next_batch, per_chunk, me_ref, *refs):
    blocks, refs = refs[:parts], refs[parts:]
    sources = ()
    if next_batch is not None:
        sources, refs = refs[:3], refs[3:]
    targets, refs = refs[:parts], refs[parts:]
    query_scr, key_scr, value_scr, out_scr, in_sems, pack_sems, out_sems = refs
    length = parts * rows
    head_width = LANES // 2
    first, second = pl.ds(0, LANES), pl.ds(LANES, LANES)

    loads = []
    for part, block in enumerate(blocks):
        here = pl.ds(part * rows, rows)
        for which, target in (
            (0, query_scr.at[here, :]),
            (1, key_scr.at[here, first]),
            (1, key_scr.at[here, second]),
            (2, value_scr.at[here, first]),
        ):
            loads.append(
                pltpu.make_async_copy(
                    block.at[pl.ds(which * rows, rows), :], target, in_sems.at[len(loads)]
                )
            )
    for copy in loads:
        copy.start()
    packs = []
    if next_batch is not None:
        packs = source_copies(me_ref[0], next_batch, per_chunk, sources, targets, pack_sems)
    for copy in packs:
        copy.start()
    value_scr[:, LANES : 2 * LANES] = jnp.ones((length, LANES), value_scr.dtype)
    for copy in loads:
        copy.wait()

    block_rows = group * rows
    lane = lax.broadcasted_iota(jnp.int32, (block_rows, 2 * LANES), 1) % LANES
    own = lax.broadcasted_iota(jnp.int32, (block_rows, LANES), 1) // head_width

    def one_block(step, carry):
        here = pl.ds(pl.multiple_of(step * block_rows, block_rows), block_rows)
        query = query_scr[here, :].astype(jnp.float32)
        query = query * (head_width ** (-0.5) * math.log2(math.e))
        high = query.astype(jnp.bfloat16)
        low = (query - high.astype(jnp.float32)).astype(jnp.bfloat16)
        pair = jnp.concatenate([high, low], axis=1)
        results = []
        for head in range(2):
            masked = jnp.where((lane // head_width) == head, pair, jnp.zeros_like(pair))
            scores = lax.dot_general(
                masked,
                key_scr[...],
                (((1,), (1,)), ((), ())),
                preferred_element_type=jnp.float32,
            )
            top = jnp.max(scores, axis=-1, keepdims=True)
            weights = jnp.exp2(scores - top).astype(jnp.bfloat16)
            total = jnp.dot(weights, value_scr[...], preferred_element_type=jnp.float32)
            results.append(total[:, 0:LANES] / total[:, LANES : 2 * LANES])
        out_scr[here, :] = jnp.where(own == 0, results[0], results[1]).astype(out_scr.dtype)
        return carry

    lax.fori_loop(0, length // block_rows, one_block, 0)
    offset = 0 if next_batch is None else 3 * rows
    stores = [
        pltpu.make_async_copy(
            out_scr.at[pl.ds(part * rows, rows), :],
            target.at[pl.ds(offset, rows), :],
            out_sems.at[part],
        )
        for part, target in enumerate(targets)
    ]
    for copy in stores:
        copy.start()
    for copy in packs + stores:
        copy.wait()


def attend(me, blocks, rows, sources, next_batch, per_chunk):
    parts = len(blocks)
    length = parts * rows
    dtype = blocks[0].dtype
    group = max(1, 256 // rows)
    extra = () if next_batch is None else tuple(sources)
    out_rows = rows if next_batch is None else 4 * rows
    anywhere = pl.BlockSpec(memory_space=pl.ANY)
    return pl.pallas_call(
        functools.partial(attend_kernel, parts, rows, group, next_batch, per_chunk),
        in_specs=[pl.BlockSpec(memory_space=pltpu.SMEM)] + [anywhere] * (parts + len(extra)),
        out_specs=[anywhere] * parts,
        out_shape=[jax.ShapeDtypeStruct((out_rows, LANES), dtype)] * parts,
        scratch_shapes=[
            pltpu.VMEM((length, LANES), dtype),
            pltpu.VMEM((length, 2 * LANES), dtype),
            pltpu.VMEM((length, 2 * LANES), dtype),
            pltpu.VMEM((length, LANES), dtype),
            pltpu.SemaphoreType.DMA((4 * parts,)),
            pltpu.SemaphoreType.DMA((3 * parts,)),
            pltpu.SemaphoreType.DMA((parts,)),
        ],
        compiler_params=pltpu.CompilerParams(vmem_limit_bytes=VMEM_LIMIT),
        cost_estimate=pl.CostEstimate(
            flops=2 * 2 * 2 * length * length * 256,
            bytes_accessed=parts * rows * LANES * 8,
            transcendentals=2 * length * length,
        ),
        name="attend",
    )(me, *blocks, *extra)


def gather_kernel(first_batch, per_chunk, parts, offset, me_ref, *refs):
    spatial_ref, piece_ref, sems = refs[-3:]
    blocks = refs[:parts]
    rows = piece_ref.shape[1]
    lane_blocks = piece_ref.shape[2] // LANES
    copies = []
    for shift, block in enumerate(blocks):
        video, lanes = block_place(me_ref[0], shift, lane_blocks, per_chunk)
        source = block.at[pl.ds(offset, rows), :]
        for target in (piece_ref.at[video, :, lanes], spatial_ref.at[first_batch + video, 0, :, lanes]):
            copies.append(pltpu.make_async_copy(source, target, sems.at[len(copies)]))
    for copy in copies:
        copy.start()
    for copy in copies:
        copy.wait()


def gather(me, carry, blocks, offset, shape, first_batch, per_chunk):
    parts = len(blocks)
    batch_size, single, rows, width = shape.shape
    anywhere = pl.BlockSpec(memory_space=pl.ANY)
    return pl.pallas_call(
        functools.partial(gather_kernel, first_batch, per_chunk, parts, offset),
        in_specs=[pl.BlockSpec(memory_space=pltpu.SMEM)] + [anywhere] * (parts + len(carry)),
        out_specs=[anywhere] * 2,
        out_shape=[shape, jax.ShapeDtypeStruct((per_chunk, rows, width), shape.dtype)],
        scratch_shapes=[pltpu.SemaphoreType.DMA((2 * parts,))],
        input_output_aliases={1 + parts: 0} if carry else {},
        cost_estimate=pl.CostEstimate(
            flops=0, bytes_accessed=parts * rows * LANES * 8, transcendentals=0
        ),
        name="gather",
    )(me, *blocks, *carry)


def combine_kernel(views, group, carried, *refs):
    refs = refs[carried:]
    query_ref = refs[0]
    key_refs = refs[1 : 1 + views]
    value_refs = refs[1 + views : 1 + 2 * views]
    (joined_ref,) = refs[1 + 2 * views :]
    head_width = LANES // 2
    source = (lax.broadcasted_iota(jnp.int32, (2 * LANES, LANES), 0) % LANES) // head_width
    target = lax.broadcasted_iota(jnp.int32, (2 * LANES, LANES), 1) // head_width
    spread = jnp.where(source == target, 1.0, 0.0).astype(jnp.bfloat16)
    for j in range(group):
        lanes = slice(j * LANES, (j + 1) * LANES)
        query = query_ref[0, 0, :, lanes].astype(jnp.float32)
        scores = []
        for key_ref in key_refs:
            product = query * key_ref[0, 0, :, lanes].astype(jnp.float32)
            high = product.astype(jnp.bfloat16)
            low = (product - high.astype(jnp.float32)).astype(jnp.bfloat16)
            both = jnp.concatenate([high, low], axis=1)
            scores.append(
                jnp.dot(both, spread, preferred_element_type=jnp.float32)
                * (head_width ** (-0.5))
            )
        top = functools.reduce(jnp.maximum, scores)
        expo = [jnp.exp(score - top) for score in scores]
        inverse = 1.0 / functools.reduce(jnp.add, expo)
        joined = None
        for value_ref, part in zip(value_refs, expo):
            weight = (part * inverse).astype(jnp.bfloat16).astype(jnp.float32)
            term = weight * value_ref[0, :, lanes].astype(jnp.float32)
            joined = term if joined is None else joined + term
        joined_ref[0, 0, :, lanes] = joined.astype(joined_ref.dtype)


def combine(carry, view_queries, keys, outputs, first_batch):
    batch_size, single, rows, width = view_queries.shape
    per_chunk = outputs[0].shape[0]
    views = len(keys)
    group = 4
    steps = width // LANES // group

    def place(i):
        return (first_batch + i // steps, 0, 0, i % steps)

    wide = pl.BlockSpec((1, 1, rows, group * LANES), place)
    narrow = pl.BlockSpec((1, rows, group * LANES), lambda i: (i // steps, 0, i % steps))
    shape = jax.ShapeDtypeStruct(view_queries.shape, view_queries.dtype)
    carried = len(carry)
    size = per_chunk * rows * width
    return pl.pallas_call(
        functools.partial(combine_kernel, views, group, carried),
        grid=(per_chunk * steps,),
        in_specs=[pl.BlockSpec(memory_space=pl.ANY)] * carried
        + [wide] * (1 + views)
        + [narrow] * views,
        out_specs=[wide],
        out_shape=[shape],
        input_output_aliases={i: i for i in range(carried)},
        cost_estimate=pl.CostEstimate(
            flops=size * 1024 * views,
            bytes_accessed=size * 2 * (2 * views + 2),
            transcendentals=size * (views + 1),
        ),
        name="combine",
    )(*carry, view_queries, *keys, *outputs)


def across(value, views):
    return [
        lax.ppermute(value, "view", [(i, i ^ shift) for i in range(views)])
        for shift in range(1, views)
    ]


def exchange(blocks):
    parts = len(blocks)
    arrived = [blocks[0]] + [None] * (parts - 1)
    for shift in reversed(range(1, parts)):
        arrived[shift] = lax.ppermute(
            blocks[shift], "seq", [(i, i ^ shift) for i in range(parts)]
        )
    return arrived


def local(seq_size, views, queries, key_rows, value_rows, view_queries):
    batch_size, single, rows, width = queries.shape
    per_chunk = seq_size // (width // LANES)
    chunks = batch_size // per_chunk
    ahead = 2
    me = lax.axis_index("seq").astype(jnp.int32).reshape(1)
    sources = (queries, key_rows, value_rows)
    received = {}
    for c in range(min(ahead, chunks)):
        received[c] = exchange(pack(me, sources, c * per_chunk, per_chunk, seq_size))
    other_keys = across(key_rows, views)
    received[0], other_keys = lax.optimization_barrier((received[0], other_keys))
    keys = [key_rows] + other_keys
    shape = jax.ShapeDtypeStruct(queries.shape, queries.dtype)
    spatial, joined = (), ()
    for c in range(chunks):
        later = c + ahead if c + ahead < chunks else None
        next_batch = None if later is None else later * per_chunk
        returned = exchange(attend(me, received[c], rows, sources, next_batch, per_chunk))
        if later is not None:
            received[later] = returned
        offset = 0 if later is None else 3 * rows
        spatial, piece = gather(me, spatial, returned, offset, shape, c * per_chunk, per_chunk)
        spatial = (spatial,)
        outputs = [piece] + across(piece, views)
        joined = combine(joined, view_queries, keys, outputs, c * per_chunk)
    return spatial[0], joined[0]


def solution(mesh):
    spec = P(None, "view", "seq", None)
    return jax.shard_map(
        functools.partial(local, mesh.shape["seq"], mesh.shape["view"]),
        mesh=mesh,
        in_specs=(spec,) * 4,
        out_specs=(spec, spec),
        check_vma=False,
    )
```

```python
import functools
import math

import jax
import jax.numpy as jnp
from jax import lax
from jax.experimental import pallas as pl
from jax.experimental.pallas import tpu as pltpu
from jax.sharding import PartitionSpec as P

HEADS = 32
LANES = 128
VMEM_LIMIT = 48 * 1024 * 1024


def split_size(parts):
    return 1 << ((parts.bit_length() - 1) // 2)


def distances(me, near, far_first, outer, inner):
    shift_high, shift_low = (outer, inner) if far_first else (inner, outer)
    return (me // near ^ shift_high) * near + (me % near ^ shift_low)


def pack_kernel(near, far_first, per_chunk, rows, ahead, me_ref, *refs):
    sources, out_refs = refs[:3], refs[3 + ahead :]
    lane_blocks = sources[0].shape[3] // LANES
    for outer, out_ref in enumerate(out_refs):
        for inner in range(out_ref.shape[0]):
            block = distances(me_ref[0], near, far_first, outer, inner)
            video = 0 if per_chunk == 1 else block // lane_blocks
            column = block if per_chunk == 1 else block % lane_blocks
            lanes = pl.ds(pl.multiple_of(column * LANES, LANES), LANES)
            for which, source in enumerate(sources):
                here = slice(which * rows, (which + 1) * rows)
                out_ref[inner, here, :] = source[video, 0, :, lanes]


def pack(me, sources, first_batch, per_chunk, parts, far_first, after=()):
    batch_size, single, rows, width = sources[0].shape
    near = split_size(parts)
    count = parts // near if far_first else near
    spec = pl.BlockSpec(
        (per_chunk, 1, rows, width), lambda i: (first_batch // per_chunk, 0, 0, 0)
    )
    shape = (parts // count, 3 * rows, LANES)
    return pl.pallas_call(
        functools.partial(pack_kernel, near, far_first, per_chunk, rows, len(after)),
        grid=(1,),
        in_specs=[pl.BlockSpec(memory_space=pltpu.SMEM)]
        + [spec] * 3
        + [pl.BlockSpec(memory_space=pl.ANY)] * len(after),
        out_specs=[pl.BlockSpec(shape, lambda i: (0, 0, 0))] * count,
        out_shape=[jax.ShapeDtypeStruct(shape, sources[0].dtype)] * count,
        cost_estimate=pl.CostEstimate(
            flops=0, bytes_accessed=parts * 3 * rows * LANES * 4, transcendentals=0
        ),
        name="pack",
    )(me, *sources, *after)


def repack_kernel(count, *refs):
    in_refs, out_refs = refs[:count], refs[count:]
    for outer, out_ref in enumerate(out_refs):
        for inner, in_ref in enumerate(in_refs):
            out_ref[inner] = in_ref[outer]


def repack(blocks):
    count = len(blocks)
    far, rows, lanes = blocks[0].shape
    shape = (count, rows, lanes)
    return pl.pallas_call(
        functools.partial(repack_kernel, count),
        out_shape=[jax.ShapeDtypeStruct(shape, blocks[0].dtype)] * far,
        cost_estimate=pl.CostEstimate(
            flops=0, bytes_accessed=count * far * rows * lanes * 4, transcendentals=0
        ),
        name="repack",
    )(*blocks)


def attend_kernel(group, rows, parts, near, far_first, count, me_ref, *refs):
    in_refs = refs[:count]
    out_ref, query_scr, key_scr, value_scr = refs[-4:]
    step = pl.program_id(0)
    length = parts * rows
    head_width = LANES // 2

    def load(in_ref, index, place):
        here = pl.ds(pl.multiple_of(place * rows, rows), rows)
        query_scr[here, :] = in_ref[index, 0:rows, :]
        keys = in_ref[index, rows : 2 * rows, :]
        key_scr[here, 0:LANES] = keys
        key_scr[here, LANES : 2 * LANES] = keys
        value_scr[here, 0:LANES] = in_ref[index, 2 * rows : 3 * rows, :]

    @pl.when(step == 0)
    def _():
        value_scr[:, LANES : 2 * LANES] = jnp.ones((length, LANES), value_scr.dtype)
        for outer, in_ref in enumerate(in_refs):
            for inner in range(in_ref.shape[0]):
                load(in_ref, inner, distances(me_ref[0], near, far_first, outer, inner))

    block = group * rows
    here = pl.ds(pl.multiple_of(step * block, block), block)
    query = query_scr[here, :].astype(jnp.float32)
    query = query * (head_width ** (-0.5) * math.log2(math.e))
    high = query.astype(jnp.bfloat16)
    low = (query - high.astype(jnp.float32)).astype(jnp.bfloat16)
    pair = jnp.concatenate([high, low], axis=1)
    lane = lax.broadcasted_iota(jnp.int32, (block, 2 * LANES), 1) % LANES
    results = []
    for head in range(2):
        mine = (lane // head_width) == head
        masked = jnp.where(mine, pair, jnp.zeros_like(pair))
        scores = lax.dot_general(
            masked, key_scr[...], (((1,), (1,)), ((), ())), preferred_element_type=jnp.float32
        )
        top = jnp.max(scores, axis=-1, keepdims=True)
        weights = jnp.exp2(scores - top).astype(jnp.bfloat16)
        total = jnp.dot(weights, value_scr[...], preferred_element_type=jnp.float32)
        results.append(total[:, 0:LANES] / total[:, LANES : 2 * LANES])
    own = lax.broadcasted_iota(jnp.int32, (block, LANES), 1) // head_width
    merged = jnp.where(own == 0, results[0], results[1]).astype(out_ref.dtype)
    out_ref[...] = merged.reshape(group, rows, LANES)


def attend(me, arrived, parts, far_first, after=()):
    triple = arrived[0].shape[1]
    rows = triple // 3
    length = parts * rows
    dtype = arrived[0].dtype
    group = max(1, 256 // rows)
    count = len(arrived)
    return pl.pallas_call(
        functools.partial(
            attend_kernel, group, rows, parts, split_size(parts), far_first, count
        ),
        grid=(parts // group,),
        in_specs=[pl.BlockSpec(memory_space=pltpu.SMEM)]
        + [pl.BlockSpec(value.shape, lambda i: (0, 0, 0)) for value in arrived]
        + [pl.BlockSpec(memory_space=pl.ANY)] * len(after),
        out_specs=pl.BlockSpec((group, rows, LANES), lambda i: (i, 0, 0)),
        out_shape=jax.ShapeDtypeStruct((parts, rows, LANES), dtype),
        scratch_shapes=[
            pltpu.VMEM((length, LANES), dtype),
            pltpu.VMEM((length, 2 * LANES), dtype),
            pltpu.VMEM((length, 2 * LANES), dtype),
        ],
        compiler_params=pltpu.CompilerParams(vmem_limit_bytes=VMEM_LIMIT),
        cost_estimate=pl.CostEstimate(
            flops=2 * 2 * 2 * length * length * 256,
            bytes_accessed=parts * rows * LANES * 8,
            transcendentals=2 * length * length,
        ),
        name="attend",
    )(me, *arrived, *after)


def combine_kernel(views, group, carried, view_ref, *refs):
    refs = refs[carried:]
    query_ref = refs[0]
    key_refs = refs[1 : 1 + views]
    value_refs = refs[1 + views : 1 + 2 * views]
    spatial_ref, joined_ref = refs[1 + 2 * views :]
    head_width = LANES // 2
    source = (lax.broadcasted_iota(jnp.int32, (2 * LANES, LANES), 0) % LANES) // head_width
    target = lax.broadcasted_iota(jnp.int32, (2 * LANES, LANES), 1) // head_width
    spread = jnp.where(source == target, 1.0, 0.0).astype(jnp.bfloat16)
    for j in range(group):
        lanes = slice(j * LANES, (j + 1) * LANES)
        query = query_ref[0, 0, :, lanes].astype(jnp.float32)
        scores = []
        for key_ref in key_refs:
            product = query * key_ref[0, 0, 0, :, lanes].astype(jnp.float32)
            high = product.astype(jnp.bfloat16)
            low = (product - high.astype(jnp.float32)).astype(jnp.bfloat16)
            both = jnp.concatenate([high, low], axis=1)
            scores.append(
                jnp.dot(both, spread, preferred_element_type=jnp.float32)
                * (head_width ** (-0.5))
            )
        top = functools.reduce(jnp.maximum, scores)
        expo = [jnp.exp(score - top) for score in scores]
        inverse = 1.0 / functools.reduce(jnp.add, expo)
        joined = None
        for value_ref, part in zip(value_refs, expo):
            weight = (part * inverse).astype(jnp.bfloat16).astype(jnp.float32)
            term = weight * value_ref[j].astype(jnp.float32)
            joined = term if joined is None else joined + term
        joined_ref[0, 0, :, lanes] = joined.astype(joined_ref.dtype)
        spatial_ref[0, 0, :, lanes] = value_refs[0][j]


def combine(view, carry, view_queries, keys, outputs, first_batch):
    batch_size, single, rows, width = view_queries.shape
    parts = outputs[0].shape[0]
    views = len(outputs)
    group = 4
    steps = width // LANES // group

    def place(i, view_ref):
        return (first_batch + i // steps, 0, 0, i % steps)

    def key_place(shift, i, view_ref):
        return (view_ref[0] ^ shift,) + place(i, view_ref)

    wide = pl.BlockSpec((1, 1, rows, group * LANES), place)
    key_specs = [
        pl.BlockSpec((1, 1, 1, rows, group * LANES), functools.partial(key_place, shift))
        for shift in range(views)
    ]
    narrow = pl.BlockSpec((group, rows, LANES), lambda i, view_ref: (i, 0, 0))
    shape = jax.ShapeDtypeStruct(view_queries.shape, view_queries.dtype)
    carried = len(carry)
    return pl.pallas_call(
        functools.partial(combine_kernel, views, group, carried),
        grid_spec=pltpu.PrefetchScalarGridSpec(
            num_scalar_prefetch=1,
            grid=(parts // group,),
            in_specs=[pl.BlockSpec(memory_space=pl.ANY)] * carried
            + [wide]
            + key_specs
            + [narrow] * views,
            out_specs=[wide, wide],
        ),
        out_shape=[shape, shape],
        input_output_aliases={1 + i: i for i in range(carried)},
        cost_estimate=pl.CostEstimate(
            flops=parts * rows * LANES * 1024 * views,
            bytes_accessed=parts * rows * LANES * 2 * (2 * views + 3),
            transcendentals=parts * rows * LANES * (views + 1),
        ),
        name="combine",
    )(view, *carry, view_queries, *[keys] * views, *outputs)


def swap(blocks, axis, size, stride):
    return [blocks[0]] + [
        lax.ppermute(blocks[shift], axis, [(i, i ^ (shift * stride)) for i in range(size)])
        for shift in range(1, len(blocks))
    ]


def local(seq_size, views, queries, key_rows, value_rows, view_queries):
    batch_size, single, rows, width = queries.shape
    per_chunk = seq_size // (width // LANES)
    chunks = batch_size // per_chunk
    near = split_size(seq_size)
    me = lax.axis_index("seq").astype(jnp.int32).reshape(1)
    view = lax.axis_index("view").astype(jnp.int32).reshape(1)
    exchange = functools.partial(
        lax.all_to_all, axis_name="seq", split_axis=0, concat_axis=0, tiled=True
    )
    keys = lax.all_gather(key_rows, "view")
    sources = (queries, key_rows, value_rows)
    received, first_packed, after = [], [], ()
    for c in range(chunks):
        strides = (near, 1) if c == 0 else (1, near)
        packed = pack(me, sources, c * per_chunk, per_chunk, seq_size, c == 0, after)
        first_packed.append(packed[0])
        blocks = repack(swap(packed, "seq", seq_size, strides[0]))
        after = (packed[0],) if c == 0 else (blocks[0],)
        received.append(swap(blocks, "seq", seq_size, strides[1]))
    carry, attended = (), ()
    for c in range(chunks):
        after = attended + tuple(first_packed[c + 2 : c + 3])
        if c == 1:
            after += (keys,)
        attended = (attend(me, received[c], seq_size, c > 0, after),)
        returned = exchange(attended[0])
        outputs = swap([returned] * views, "view", views, 1)
        carry = combine(view, carry, view_queries, keys, outputs, c * per_chunk)
    return tuple(carry)


def solution(mesh):
    spec = P(None, "view", "seq", None)
    return jax.shard_map(
        functools.partial(local, mesh.shape["seq"], mesh.shape["view"]),
        mesh=mesh,
        in_specs=(spec,) * 4,
        out_specs=(spec, spec),
        check_vma=False,
    )
```

```python
import functools
import math

import jax
import jax.numpy as jnp
from jax import lax
from jax.experimental import pallas as pl
from jax.experimental.pallas import tpu as pltpu
from jax.sharding import PartitionSpec as P

HEADS = 32
LANES = 128
VMEM_LIMIT = 48 * 1024 * 1024


def split_size(parts):
    return 1 << ((parts.bit_length() - 1) // 2)


def pack_kernel(near, per_chunk, rows, ahead, me_ref, *refs):
    sources, out_refs = refs[:3], refs[3 + ahead :]
    lane_blocks = sources[0].shape[3] // LANES
    high = me_ref[0] // near
    for shift, out_ref in enumerate(out_refs):
        for low in range(near):
            block = (high ^ shift) * near + low
            video = 0 if per_chunk == 1 else block // lane_blocks
            column = block if per_chunk == 1 else block % lane_blocks
            lanes = pl.ds(pl.multiple_of(column * LANES, LANES), LANES)
            for which, source in enumerate(sources):
                here = slice(which * rows, (which + 1) * rows)
                out_ref[low, here, :] = source[video, 0, :, lanes]


def pack(me, sources, first_batch, per_chunk, parts, after=()):
    batch_size, single, rows, width = sources[0].shape
    near = split_size(parts)
    far = parts // near
    spec = pl.BlockSpec(
        (per_chunk, 1, rows, width), lambda i: (first_batch // per_chunk, 0, 0, 0)
    )
    shape = (near, 3 * rows, LANES)
    return pl.pallas_call(
        functools.partial(pack_kernel, near, per_chunk, rows, len(after)),
        grid=(1,),
        in_specs=[pl.BlockSpec(memory_space=pltpu.SMEM)]
        + [spec] * 3
        + [pl.BlockSpec(memory_space=pl.ANY)] * len(after),
        out_specs=[pl.BlockSpec(shape, lambda i: (0, 0, 0))] * far,
        out_shape=[jax.ShapeDtypeStruct(shape, sources[0].dtype)] * far,
        cost_estimate=pl.CostEstimate(
            flops=0, bytes_accessed=parts * 3 * rows * LANES * 4, transcendentals=0
        ),
        name="pack",
    )(me, *sources, *after)


def repack_kernel(near, far, ahead, me_ref, *refs):
    in_refs, out_refs = refs[:far], refs[far + ahead :]
    low = me_ref[0] % near
    for shift, in_ref in enumerate(in_refs):
        for other in range(near):
            if len(out_refs) == 1:
                out_refs[0][other, shift] = in_ref[other]
            else:
                out_refs[other][shift] = in_ref[low ^ other]


def repack(me, blocks, single, after=()):
    far = len(blocks)
    near, rows, lanes = blocks[0].shape
    shape, count = ((near, far, rows, lanes), 1) if single else ((far, rows, lanes), near)
    return pl.pallas_call(
        functools.partial(repack_kernel, near, far, len(after)),
        in_specs=[pl.BlockSpec(memory_space=pltpu.SMEM)]
        + [pl.BlockSpec(memory_space=pltpu.VMEM)] * far
        + [pl.BlockSpec(memory_space=pl.ANY)] * len(after),
        out_shape=[jax.ShapeDtypeStruct(shape, blocks[0].dtype)] * count,
        cost_estimate=pl.CostEstimate(
            flops=0, bytes_accessed=near * far * rows * lanes * 4, transcendentals=0
        ),
        name="repack",
    )(me, *blocks, *after)


def attend_kernel(group, rows, parts, near, count, me_ref, *refs):
    in_refs = refs[:count]
    out_ref, query_scr, key_scr, value_scr = refs[-4:]
    step = pl.program_id(0)
    length = parts * rows
    head_width = LANES // 2

    def load(in_ref, index, place):
        here = pl.ds(pl.multiple_of(place * rows, rows), rows)
        query_scr[here, :] = in_ref[index, 0:rows, :]
        keys = in_ref[index, rows : 2 * rows, :]
        key_scr[here, 0:LANES] = keys
        key_scr[here, LANES : 2 * LANES] = keys
        value_scr[here, 0:LANES] = in_ref[index, 2 * rows : 3 * rows, :]

    @pl.when(step == 0)
    def _():
        value_scr[:, LANES : 2 * LANES] = jnp.ones((length, LANES), value_scr.dtype)
        high, low = me_ref[0] // near, me_ref[0] % near
        for shift in range(parts // near):
            for other in range(near):
                if count == 1:
                    load(in_refs[0].at[other], shift, (high ^ shift) * near + other)
                else:
                    load(in_refs[other], shift, (high ^ shift) * near + (low ^ other))

    block = group * rows
    here = pl.ds(pl.multiple_of(step * block, block), block)
    query = query_scr[here, :].astype(jnp.float32)
    query = query * (head_width ** (-0.5) * math.log2(math.e))
    high = query.astype(jnp.bfloat16)
    low = (query - high.astype(jnp.float32)).astype(jnp.bfloat16)
    pair = jnp.concatenate([high, low], axis=1)
    lane = lax.broadcasted_iota(jnp.int32, (block, 2 * LANES), 1) % LANES
    results = []
    for head in range(2):
        mine = (lane // head_width) == head
        masked = jnp.where(mine, pair, jnp.zeros_like(pair))
        scores = lax.dot_general(
            masked, key_scr[...], (((1,), (1,)), ((), ())), preferred_element_type=jnp.float32
        )
        top = jnp.max(scores, axis=-1, keepdims=True)
        weights = jnp.exp2(scores - top).astype(jnp.bfloat16)
        total = jnp.dot(weights, value_scr[...], preferred_element_type=jnp.float32)
        results.append(total[:, 0:LANES] / total[:, LANES : 2 * LANES])
    own = lax.broadcasted_iota(jnp.int32, (block, LANES), 1) // head_width
    merged = jnp.where(own == 0, results[0], results[1]).astype(out_ref.dtype)
    out_ref[...] = merged.reshape(group, rows, LANES)


def attend(me, arrived, parts, after=()):
    triple = arrived[0].shape[-2]
    rows = triple // 3
    length = parts * rows
    dtype = arrived[0].dtype
    group = max(1, 512 // rows)
    count = len(arrived)
    return pl.pallas_call(
        functools.partial(attend_kernel, group, rows, parts, split_size(parts), count),
        grid=(parts // group,),
        in_specs=[pl.BlockSpec(memory_space=pltpu.SMEM)]
        + [pl.BlockSpec(value.shape, lambda i, n=value.ndim: (0,) * n) for value in arrived]
        + [pl.BlockSpec(memory_space=pl.ANY)] * len(after),
        out_specs=pl.BlockSpec((group, rows, LANES), lambda i: (i, 0, 0)),
        out_shape=jax.ShapeDtypeStruct((parts, rows, LANES), dtype),
        scratch_shapes=[
            pltpu.VMEM((length, LANES), dtype),
            pltpu.VMEM((length, 2 * LANES), dtype),
            pltpu.VMEM((length, 2 * LANES), dtype),
        ],
        compiler_params=pltpu.CompilerParams(vmem_limit_bytes=VMEM_LIMIT),
        cost_estimate=pl.CostEstimate(
            flops=2 * 2 * 2 * length * length * 256,
            bytes_accessed=parts * rows * LANES * 8,
            transcendentals=2 * length * length,
        ),
        name="attend",
    )(me, *arrived, *after)


def combine_kernel(views, group, carried, view_ref, *refs):
    refs = refs[carried:]
    query_ref = refs[0]
    key_refs = refs[1 : 1 + views]
    value_refs = refs[1 + views : 1 + 2 * views]
    spatial_ref, joined_ref = refs[1 + 2 * views :]
    head_width = LANES // 2
    source = (lax.broadcasted_iota(jnp.int32, (2 * LANES, LANES), 0) % LANES) // head_width
    target = lax.broadcasted_iota(jnp.int32, (2 * LANES, LANES), 1) // head_width
    spread = jnp.where(source == target, 1.0, 0.0).astype(jnp.bfloat16)
    for j in range(group):
        lanes = slice(j * LANES, (j + 1) * LANES)
        query = query_ref[0, 0, :, lanes].astype(jnp.float32)
        scores = []
        for key_ref in key_refs:
            product = query * key_ref[0, 0, 0, :, lanes].astype(jnp.float32)
            high = product.astype(jnp.bfloat16)
            low = (product - high.astype(jnp.float32)).astype(jnp.bfloat16)
            both = jnp.concatenate([high, low], axis=1)
            scores.append(
                jnp.dot(both, spread, preferred_element_type=jnp.float32)
                * (head_width ** (-0.5))
            )
        top = functools.reduce(jnp.maximum, scores)
        expo = [jnp.exp(score - top) for score in scores]
        inverse = 1.0 / functools.reduce(jnp.add, expo)
        joined = None
        for value_ref, part in zip(value_refs, expo):
            weight = (part * inverse).astype(jnp.bfloat16).astype(jnp.float32)
            term = weight * value_ref[0, j].astype(jnp.float32)
            joined = term if joined is None else joined + term
        joined_ref[0, 0, :, lanes] = joined.astype(joined_ref.dtype)
        spatial_ref[0, 0, :, lanes] = value_refs[0][0, j]


def combine(view, carry, view_queries, keys, outputs, first_batch):
    batch_size, single, rows, width = view_queries.shape
    parts = outputs[0].shape[-3]
    views = len(outputs)
    group = 4
    steps = width // LANES // group

    def place(i, view_ref):
        return (first_batch + i // steps, 0, 0, i % steps)

    def key_place(shift, i, view_ref):
        return (view_ref[0] ^ shift,) + place(i, view_ref)

    wide = pl.BlockSpec((1, 1, rows, group * LANES), place)
    key_specs = [
        pl.BlockSpec((1, 1, 1, rows, group * LANES), functools.partial(key_place, shift))
        for shift in range(views)
    ]

    def output_place(shift, i, view_ref):
        return (view_ref[0] ^ shift if outputs[shift].shape[0] > 1 else 0, i, 0, 0)

    output_specs = [
        pl.BlockSpec((1, group, rows, LANES), functools.partial(output_place, shift))
        for shift in range(views)
    ]
    shape = jax.ShapeDtypeStruct(view_queries.shape, view_queries.dtype)
    carried = len(carry)
    return pl.pallas_call(
        functools.partial(combine_kernel, views, group, carried),
        grid_spec=pltpu.PrefetchScalarGridSpec(
            num_scalar_prefetch=1,
            grid=(parts // group,),
            in_specs=[pl.BlockSpec(memory_space=pl.ANY)] * carried
            + [wide]
            + key_specs
            + output_specs,
            out_specs=[wide, wide],
        ),
        out_shape=[shape, shape],
        input_output_aliases={1 + i: i for i in range(carried)},
        cost_estimate=pl.CostEstimate(
            flops=parts * rows * LANES * 1024 * views,
            bytes_accessed=parts * rows * LANES * 2 * (2 * views + 3),
            transcendentals=parts * rows * LANES * (views + 1),
        ),
        name="combine",
    )(view, *carry, view_queries, *[keys] * views, *outputs)


def swap(blocks, axis, size, stride):
    arrived = list(blocks)
    for shift in reversed(range(1, len(blocks))):
        arrived[shift] = lax.ppermute(
            blocks[shift], axis, [(i, i ^ (shift * stride)) for i in range(size)]
        )
    return arrived


def local(seq_size, views, queries, key_rows, value_rows, view_queries):
    batch_size, single, rows, width = queries.shape
    per_chunk = seq_size // (width // LANES)
    chunks = batch_size // per_chunk
    near = split_size(seq_size)
    me = lax.axis_index("seq").astype(jnp.int32).reshape(1)
    view = lax.axis_index("view").astype(jnp.int32).reshape(1)
    exchange = functools.partial(
        lax.all_to_all, axis_name="seq", split_axis=0, concat_axis=0, tiled=True
    )
    neighbours = [list(range(i, i + near)) for i in range(0, seq_size, near)]
    keys = lax.all_gather(key_rows, "view")
    sources = (queries, key_rows, value_rows)
    packed, crossed, received = [], [], []
    for c in range(chunks):
        after = tuple(blocks[0] for blocks in packed[-1:])
        packed.append(pack(me, sources, c * per_chunk, per_chunk, seq_size, after))
        crossed.append(swap(packed[c], "seq", seq_size, near))
    repacked, received = [], []

    def arrive(c, after):
        repacked.append(repack(me, crossed[c], 2 * c < chunks, after))
        if 2 * c < chunks:
            received.append([exchange(repacked[c][0], axis_index_groups=neighbours)])
        else:
            received.append(swap(repacked[c], "seq", seq_size, 1))

    arrive(0, ())
    carry, attended = (), ()
    for c in range(chunks):
        after = attended + tuple(blocks[1] for blocks in crossed[c + 1 : c + 2])
        if c + 1 < chunks - 1:
            arrive(c + 1, attended or (repacked[0][0],))
            after += (repacked[c + 1][0],)
        if c == 1:
            after += (keys,)
        attended = (attend(me, received[c], seq_size, after),)
        if c + 1 == chunks - 1:
            arrive(c + 1, attended)
        returned = exchange(attended[0])
        own = returned[None]
        if c + 2 < chunks:
            outputs = [own] + [lax.all_gather(returned, "view")] * (views - 1)
        else:
            outputs = swap([own] * views, "view", views, 1)
        carry = combine(view, carry, view_queries, keys, outputs, c * per_chunk)
    return tuple(carry)


def solution(mesh):
    spec = P(None, "view", "seq", None)
    return jax.shard_map(
        functools.partial(local, mesh.shape["seq"], mesh.shape["view"]),
        mesh=mesh,
        in_specs=(spec,) * 4,
        out_specs=(spec, spec),
        check_vma=False,
    )
```

```python
import functools
import math

import jax
import jax.numpy as jnp
from jax import lax
from jax.experimental import pallas as pl
from jax.experimental.pallas import tpu as pltpu
from jax.sharding import PartitionSpec as P

HEADS = 32
LANES = 128
VMEM_LIMIT = 48 * 1024 * 1024


def split_size(parts):
    return 1 << ((parts.bit_length() - 1) // 2)


def pack_kernel(near, per_chunk, rows, ahead, me_ref, *refs):
    sources, out_refs = refs[:3], refs[3 + ahead :]
    lane_blocks = sources[0].shape[3] // LANES
    high = me_ref[0] // near
    single = len(out_refs) == 1
    far = out_refs[0].shape[1] if single else len(out_refs)
    for shift in range(far):
        for low in range(near):
            target = out_refs[0].at[low, shift] if single else out_refs[shift].at[low]
            block = (high ^ shift) * near + low
            video = 0 if per_chunk == 1 else block // lane_blocks
            column = block if per_chunk == 1 else block % lane_blocks
            lanes = pl.ds(pl.multiple_of(column * LANES, LANES), LANES)
            for which, source in enumerate(sources):
                here = slice(which * rows, (which + 1) * rows)
                target[here, :] = source[video, 0, :, lanes]


def pack(me, sources, first_batch, per_chunk, parts, single, after=()):
    batch_size, _, rows, width = sources[0].shape
    near = split_size(parts)
    far = parts // near
    spec = pl.BlockSpec(
        (per_chunk, 1, rows, width), lambda i: (first_batch // per_chunk, 0, 0, 0)
    )
    shape = (near, far, 3 * rows, LANES) if single else (near, 3 * rows, LANES)
    count = 1 if single else far
    return pl.pallas_call(
        functools.partial(pack_kernel, near, per_chunk, rows, len(after)),
        grid=(1,),
        in_specs=[pl.BlockSpec(memory_space=pltpu.SMEM)]
        + [spec] * 3
        + [pl.BlockSpec(memory_space=pl.ANY)] * len(after),
        out_specs=[pl.BlockSpec(shape, lambda i: (0,) * len(shape))] * count,
        out_shape=[jax.ShapeDtypeStruct(shape, sources[0].dtype)] * count,
        cost_estimate=pl.CostEstimate(
            flops=0, bytes_accessed=parts * 3 * rows * LANES * 4, transcendentals=0
        ),
        name="pack",
    )(me, *sources, *after)


def repack_kernel(near, far, ahead, me_ref, *refs):
    in_refs, out_refs = refs[:far], refs[far + ahead :]
    low = me_ref[0] % near
    for shift, in_ref in enumerate(in_refs):
        for other in range(near):
            if len(out_refs) == 1:
                out_refs[0][other, shift] = in_ref[other]
            else:
                out_refs[other][shift] = in_ref[low ^ other]


def repack(me, blocks, single, after=()):
    far = len(blocks)
    near, rows, lanes = blocks[0].shape
    shape, count = ((near, far, rows, lanes), 1) if single else ((far, rows, lanes), near)
    return pl.pallas_call(
        functools.partial(repack_kernel, near, far, len(after)),
        in_specs=[pl.BlockSpec(memory_space=pltpu.SMEM)]
        + [pl.BlockSpec(memory_space=pltpu.VMEM)] * far
        + [pl.BlockSpec(memory_space=pl.ANY)] * len(after),
        out_shape=[jax.ShapeDtypeStruct(shape, blocks[0].dtype)] * count,
        cost_estimate=pl.CostEstimate(
            flops=0, bytes_accessed=near * far * rows * lanes * 4, transcendentals=0
        ),
        name="repack",
    )(me, *blocks, *after)


def unpack_kernel(near, ahead, in_ref, *refs):
    for shift, out_ref in enumerate(refs[ahead:]):
        for other in range(near):
            out_ref[other] = in_ref[other, shift]


def unpack(block, after=()):
    near, far, rows, lanes = block.shape
    shape = (near, rows, lanes)
    return pl.pallas_call(
        functools.partial(unpack_kernel, near, len(after)),
        in_specs=[pl.BlockSpec(memory_space=pltpu.VMEM)]
        + [pl.BlockSpec(memory_space=pl.ANY)] * len(after),
        out_shape=[jax.ShapeDtypeStruct(shape, block.dtype)] * far,
        cost_estimate=pl.CostEstimate(
            flops=0, bytes_accessed=near * far * rows * lanes * 4, transcendentals=0
        ),
        name="unpack",
    )(block, *after)


def attend_kernel(group, rows, parts, near, by_far, count, me_ref, *refs):
    in_refs = refs[:count]
    out_ref, query_scr, key_scr, value_scr = refs[-4:]
    step = pl.program_id(0)
    length = parts * rows
    head_width = LANES // 2

    def load(in_ref, index, place):
        here = pl.ds(pl.multiple_of(place * rows, rows), rows)
        query_scr[here, :] = in_ref[index, 0:rows, :]
        keys = in_ref[index, rows : 2 * rows, :]
        key_scr[here, 0:LANES] = keys
        key_scr[here, LANES : 2 * LANES] = keys
        value_scr[here, 0:LANES] = in_ref[index, 2 * rows : 3 * rows, :]

    @pl.when(step == 0)
    def _():
        value_scr[:, LANES : 2 * LANES] = jnp.ones((length, LANES), value_scr.dtype)
        high, low = me_ref[0] // near, me_ref[0] % near
        for shift in range(parts // near):
            for other in range(near):
                if by_far:
                    load(in_refs[shift], other, (high ^ shift) * near + other)
                elif count == 1:
                    load(in_refs[0].at[other], shift, (high ^ shift) * near + other)
                else:
                    load(in_refs[other], shift, (high ^ shift) * near + (low ^ other))

    block = group * rows
    here = pl.ds(pl.multiple_of(step * block, block), block)
    query = query_scr[here, :].astype(jnp.float32)
    query = query * (head_width ** (-0.5) * math.log2(math.e))
    high = query.astype(jnp.bfloat16)
    low = (query - high.astype(jnp.float32)).astype(jnp.bfloat16)
    pair = jnp.concatenate([high, low], axis=1)
    lane = lax.broadcasted_iota(jnp.int32, (block, 2 * LANES), 1) % LANES
    results = []
    for head in range(2):
        mine = (lane // head_width) == head
        masked = jnp.where(mine, pair, jnp.zeros_like(pair))
        scores = lax.dot_general(
            masked, key_scr[...], (((1,), (1,)), ((), ())), preferred_element_type=jnp.float32
        )
        top = jnp.max(scores, axis=-1, keepdims=True)
        weights = jnp.exp2(scores - top).astype(jnp.bfloat16)
        total = jnp.dot(weights, value_scr[...], preferred_element_type=jnp.float32)
        results.append(total[:, 0:LANES] / total[:, LANES : 2 * LANES])
    own = lax.broadcasted_iota(jnp.int32, (block, LANES), 1) // head_width
    merged = jnp.where(own == 0, results[0], results[1]).astype(out_ref.dtype)
    out_ref[...] = merged.reshape(group, rows, LANES)


def attend(me, arrived, parts, by_far, after=()):
    triple = arrived[0].shape[-2]
    rows = triple // 3
    length = parts * rows
    dtype = arrived[0].dtype
    group = max(1, 512 // rows)
    count = len(arrived)
    return pl.pallas_call(
        functools.partial(
            attend_kernel, group, rows, parts, split_size(parts), by_far, count
        ),
        grid=(parts // group,),
        in_specs=[pl.BlockSpec(memory_space=pltpu.SMEM)]
        + [pl.BlockSpec(value.shape, lambda i, n=value.ndim: (0,) * n) for value in arrived]
        + [pl.BlockSpec(memory_space=pl.ANY)] * len(after),
        out_specs=pl.BlockSpec((group, rows, LANES), lambda i: (i, 0, 0)),
        out_shape=jax.ShapeDtypeStruct((parts, rows, LANES), dtype),
        scratch_shapes=[
            pltpu.VMEM((length, LANES), dtype),
            pltpu.VMEM((length, 2 * LANES), dtype),
            pltpu.VMEM((length, 2 * LANES), dtype),
        ],
        compiler_params=pltpu.CompilerParams(vmem_limit_bytes=VMEM_LIMIT),
        cost_estimate=pl.CostEstimate(
            flops=2 * 2 * 2 * length * length * 256,
            bytes_accessed=parts * rows * LANES * 8,
            transcendentals=2 * length * length,
        ),
        name="attend",
    )(me, *arrived, *after)


def combine_kernel(views, group, carried, view_ref, *refs):
    refs = refs[carried:]
    query_ref = refs[0]
    key_refs = refs[1 : 1 + views]
    value_refs = refs[1 + views : 1 + 2 * views]
    spatial_ref, joined_ref = refs[1 + 2 * views :]
    head_width = LANES // 2
    source = (lax.broadcasted_iota(jnp.int32, (2 * LANES, LANES), 0) % LANES) // head_width
    target = lax.broadcasted_iota(jnp.int32, (2 * LANES, LANES), 1) // head_width
    spread = jnp.where(source == target, 1.0, 0.0).astype(jnp.bfloat16)
    for j in range(group):
        lanes = slice(j * LANES, (j + 1) * LANES)
        query = query_ref[0, 0, :, lanes].astype(jnp.float32)
        scores = []
        for key_ref in key_refs:
            product = query * key_ref[0, 0, 0, :, lanes].astype(jnp.float32)
            high = product.astype(jnp.bfloat16)
            low = (product - high.astype(jnp.float32)).astype(jnp.bfloat16)
            both = jnp.concatenate([high, low], axis=1)
            scores.append(
                jnp.dot(both, spread, preferred_element_type=jnp.float32)
                * (head_width ** (-0.5))
            )
        top = functools.reduce(jnp.maximum, scores)
        expo = [jnp.exp(score - top) for score in scores]
        inverse = 1.0 / functools.reduce(jnp.add, expo)
        joined = None
        for value_ref, part in zip(value_refs, expo):
            weight = (part * inverse).astype(jnp.bfloat16).astype(jnp.float32)
            term = weight * value_ref[0, j].astype(jnp.float32)
            joined = term if joined is None else joined + term
        joined_ref[0, 0, :, lanes] = joined.astype(joined_ref.dtype)
        spatial_ref[0, 0, :, lanes] = value_refs[0][0, j]


def combine(view, carry, view_queries, keys, outputs, first_batch):
    batch_size, single, rows, width = view_queries.shape
    parts = outputs[0].shape[-3]
    views = len(outputs)
    group = 4
    steps = width // LANES // group

    def place(i, view_ref):
        return (first_batch + i // steps, 0, 0, i % steps)

    def key_place(shift, i, view_ref):
        return (view_ref[0] ^ shift,) + place(i, view_ref)

    wide = pl.BlockSpec((1, 1, rows, group * LANES), place)
    key_specs = [
        pl.BlockSpec((1, 1, 1, rows, group * LANES), functools.partial(key_place, shift))
        for shift in range(views)
    ]

    def output_place(shift, i, view_ref):
        return (view_ref[0] ^ shift if outputs[shift].shape[0] > 1 else 0, i, 0, 0)

    output_specs = [
        pl.BlockSpec((1, group, rows, LANES), functools.partial(output_place, shift))
        for shift in range(views)
    ]
    shape = jax.ShapeDtypeStruct(view_queries.shape, view_queries.dtype)
    carried = len(carry)
    return pl.pallas_call(
        functools.partial(combine_kernel, views, group, carried),
        grid_spec=pltpu.PrefetchScalarGridSpec(
            num_scalar_prefetch=1,
            grid=(parts // group,),
            in_specs=[pl.BlockSpec(memory_space=pl.ANY)] * carried
            + [wide]
            + key_specs
            + output_specs,
            out_specs=[wide, wide],
        ),
        out_shape=[shape, shape],
        input_output_aliases={1 + i: i for i in range(carried)},
        cost_estimate=pl.CostEstimate(
            flops=parts * rows * LANES * 1024 * views,
            bytes_accessed=parts * rows * LANES * 2 * (2 * views + 3),
            transcendentals=parts * rows * LANES * (views + 1),
        ),
        name="combine",
    )(view, *carry, view_queries, *[keys] * views, *outputs)


def swap(blocks, axis, size, stride):
    arrived = list(blocks)
    for shift in reversed(range(1, len(blocks))):
        arrived[shift] = lax.ppermute(
            blocks[shift], axis, [(i, i ^ (shift * stride)) for i in range(size)]
        )
    return arrived


def local(seq_size, views, queries, key_rows, value_rows, view_queries):
    batch_size, single, rows, width = queries.shape
    per_chunk = seq_size // (width // LANES)
    chunks = batch_size // per_chunk
    near = split_size(seq_size)
    me = lax.axis_index("seq").astype(jnp.int32).reshape(1)
    view = lax.axis_index("view").astype(jnp.int32).reshape(1)
    exchange = functools.partial(
        lax.all_to_all, axis_name="seq", split_axis=0, concat_axis=0, tiled=True
    )
    neighbours = [list(range(i, i + near)) for i in range(0, seq_size, near)]
    keys = lax.all_gather(key_rows, "view")
    sources = (queries, key_rows, value_rows)
    last = chunks - 1 if chunks > 1 else None

    def lay_out(c, single, after=()):
        return pack(me, sources, c * per_chunk, per_chunk, seq_size, single, after)

    crossed, first = {}, ()
    for c in range(chunks):
        if c != last:
            blocks = lay_out(c, False, first)
            first = (blocks[0],)
            crossed[c] = swap(blocks, "seq", seq_size, near)
        if c == 1 or (c == 0 and last == 1):
            (blocks,) = lay_out(last, True, first + (crossed[0][1],))
            last_blocks = unpack(exchange(blocks, axis_index_groups=neighbours))
    if last is not None:
        crossed[last] = swap(last_blocks, "seq", seq_size, near)

    repacked, received = {}, {}

    def arrive(c, after):
        if c == last:
            received[c] = crossed[c]
            return
        if c + 1 in crossed:
            after += (crossed[c + 1][1],)
        if c == 1:
            after += (last_blocks[0],)
        repacked[c] = repack(me, crossed[c], c < 2, after)
        if c < 2:
            received[c] = [exchange(repacked[c][0], axis_index_groups=neighbours)]
        else:
            received[c] = swap(repacked[c], "seq", seq_size, 1)

    arrive(0, ())
    if chunks > 1:
        arrive(1, ())
    carry, attended, first_output = (), (), ()
    for c in range(chunks):
        after = attended
        if 1 < c + 1 < chunks:
            arrive(c + 1, attended)
        if c + 1 in repacked and c > 0:
            after += (repacked[c + 1][0],)
        if c == 1:
            after += (keys,)
        if c == last and c > 1:
            after += first_output
        attended = (attend(me, received[c], seq_size, c == last, after),)
        returned = exchange(attended[0])
        own = returned[None]
        if c + 2 < chunks and c == 0:
            outputs = [own] + [lax.all_gather(returned, "view")] * (views - 1)
            first_output = tuple(outputs[1:2])
        else:
            outputs = swap([own] * views, "view", views, 1)
        carry = combine(view, carry, view_queries, keys, outputs, c * per_chunk)
    return tuple(carry)


def solution(mesh):
    spec = P(None, "view", "seq", None)
    return jax.shard_map(
        functools.partial(local, mesh.shape["seq"], mesh.shape["view"]),
        mesh=mesh,
        in_specs=(spec,) * 4,
        out_specs=(spec, spec),
        check_vma=False,
    )
```

```python
import functools
import math

import jax
import jax.numpy as jnp
from jax import lax
from jax.experimental import pallas as pl
from jax.experimental.pallas import tpu as pltpu
from jax.sharding import PartitionSpec as P

HEADS = 32
LANES = 128
VMEM_LIMIT = 48 * 1024 * 1024


def split_size(parts):
    return 1 << ((parts.bit_length() - 1) // 2)


def pack_kernel(near, per_chunk, rows, ahead, me_ref, *refs):
    sources, out_refs = refs[:3], refs[3 + ahead :]
    lane_blocks = sources[0].shape[3] // LANES
    high = me_ref[0] // near
    for shift, out_ref in enumerate(out_refs):
        for low in range(near):
            block = (high ^ shift) * near + low
            video = 0 if per_chunk == 1 else block // lane_blocks
            column = block if per_chunk == 1 else block % lane_blocks
            lanes = pl.ds(pl.multiple_of(column * LANES, LANES), LANES)
            for which, source in enumerate(sources):
                here = slice(which * rows, (which + 1) * rows)
                out_ref[low, here, :] = source[video, 0, :, lanes]


def pack(me, sources, first_batch, per_chunk, parts, after=()):
    batch_size, single, rows, width = sources[0].shape
    near = split_size(parts)
    far = parts // near
    spec = pl.BlockSpec(
        (per_chunk, 1, rows, width), lambda i: (first_batch // per_chunk, 0, 0, 0)
    )
    shape = (near, 3 * rows, LANES)
    return pl.pallas_call(
        functools.partial(pack_kernel, near, per_chunk, rows, len(after)),
        grid=(1,),
        in_specs=[pl.BlockSpec(memory_space=pltpu.SMEM)]
        + [spec] * 3
        + [pl.BlockSpec(memory_space=pl.ANY)] * len(after),
        out_specs=[pl.BlockSpec(shape, lambda i: (0, 0, 0))] * far,
        out_shape=[jax.ShapeDtypeStruct(shape, sources[0].dtype)] * far,
        cost_estimate=pl.CostEstimate(
            flops=0, bytes_accessed=parts * 3 * rows * LANES * 4, transcendentals=0
        ),
        name="pack",
    )(me, *sources, *after)


def repack_kernel(near, far, ahead, me_ref, *refs):
    in_refs, out_refs = refs[:far], refs[far + ahead :]
    low = me_ref[0] % near
    for shift, in_ref in enumerate(in_refs):
        for other in range(near):
            if len(out_refs) == 1:
                out_refs[0][other, shift] = in_ref[other]
            else:
                out_refs[other][shift] = in_ref[low ^ other]


def repack(me, blocks, single, after=()):
    far = len(blocks)
    near, rows, lanes = blocks[0].shape
    shape, count = ((near, far, rows, lanes), 1) if single else ((far, rows, lanes), near)
    return pl.pallas_call(
        functools.partial(repack_kernel, near, far, len(after)),
        in_specs=[pl.BlockSpec(memory_space=pltpu.SMEM)]
        + [pl.BlockSpec(memory_space=pltpu.VMEM)] * far
        + [pl.BlockSpec(memory_space=pl.ANY)] * len(after),
        out_shape=[jax.ShapeDtypeStruct(shape, blocks[0].dtype)] * count,
        cost_estimate=pl.CostEstimate(
            flops=0, bytes_accessed=near * far * rows * lanes * 4, transcendentals=0
        ),
        name="repack",
    )(me, *blocks, *after)


def attend_kernel(group, rows, parts, near, count, me_ref, *refs):
    in_refs = refs[:count]
    out_ref, query_scr, key_scr, value_scr = refs[-4:]
    step = pl.program_id(0)
    length = parts * rows
    head_width = LANES // 2

    def load(in_ref, index, place):
        here = pl.ds(pl.multiple_of(place * rows, rows), rows)
        query_scr[here, :] = in_ref[index, 0:rows, :]
        keys = in_ref[index, rows : 2 * rows, :]
        key_scr[here, 0:LANES] = keys
        key_scr[here, LANES : 2 * LANES] = keys
        value_scr[here, 0:LANES] = in_ref[index, 2 * rows : 3 * rows, :]

    @pl.when(step == 0)
    def _():
        value_scr[:, LANES : 2 * LANES] = jnp.ones((length, LANES), value_scr.dtype)
        high, low = me_ref[0] // near, me_ref[0] % near
        for shift in range(parts // near):
            for other in range(near):
                if count == 1:
                    load(in_refs[0].at[other], shift, (high ^ shift) * near + other)
                else:
                    load(in_refs[other], shift, (high ^ shift) * near + (low ^ other))

    block = group * rows
    here = pl.ds(pl.multiple_of(step * block, block), block)
    query = query_scr[here, :].astype(jnp.float32)
    query = query * (head_width ** (-0.5) * math.log2(math.e))
    high = query.astype(jnp.bfloat16)
    low = (query - high.astype(jnp.float32)).astype(jnp.bfloat16)
    pair = jnp.concatenate([high, low], axis=1)
    lane = lax.broadcasted_iota(jnp.int32, (block, 2 * LANES), 1) % LANES
    results = []
    for head in range(2):
        mine = (lane // head_width) == head
        masked = jnp.where(mine, pair, jnp.zeros_like(pair))
        scores = lax.dot_general(
            masked, key_scr[...], (((1,), (1,)), ((), ())), preferred_element_type=jnp.float32
        )
        top = jnp.max(scores, axis=-1, keepdims=True)
        weights = jnp.exp2(scores - top).astype(jnp.bfloat16)
        total = jnp.dot(weights, value_scr[...], preferred_element_type=jnp.float32)
        results.append(total[:, 0:LANES] / total[:, LANES : 2 * LANES])
    own = lax.broadcasted_iota(jnp.int32, (block, LANES), 1) // head_width
    merged = jnp.where(own == 0, results[0], results[1]).astype(out_ref.dtype)
    out_ref[...] = merged.reshape(group, rows, LANES)


def attend(me, arrived, parts, after=()):
    triple = arrived[0].shape[-2]
    rows = triple // 3
    length = parts * rows
    dtype = arrived[0].dtype
    group = max(1, 512 // rows)
    count = len(arrived)
    return pl.pallas_call(
        functools.partial(attend_kernel, group, rows, parts, split_size(parts), count),
        grid=(parts // group,),
        in_specs=[pl.BlockSpec(memory_space=pltpu.SMEM)]
        + [pl.BlockSpec(value.shape, lambda i, n=value.ndim: (0,) * n) for value in arrived]
        + [pl.BlockSpec(memory_space=pl.ANY)] * len(after),
        out_specs=pl.BlockSpec((group, rows, LANES), lambda i: (i, 0, 0)),
        out_shape=jax.ShapeDtypeStruct((parts, rows, LANES), dtype),
        scratch_shapes=[
            pltpu.VMEM((length, LANES), dtype),
            pltpu.VMEM((length, 2 * LANES), dtype),
            pltpu.VMEM((length, 2 * LANES), dtype),
        ],
        compiler_params=pltpu.CompilerParams(vmem_limit_bytes=VMEM_LIMIT),
        cost_estimate=pl.CostEstimate(
            flops=2 * 2 * 2 * length * length * 256,
            bytes_accessed=parts * rows * LANES * 8,
            transcendentals=2 * length * length,
        ),
        name="attend",
    )(me, *arrived, *after)


def combine_kernel(views, group, carried, view_ref, *refs):
    refs = refs[carried:]
    query_ref = refs[0]
    key_refs = refs[1 : 1 + views]
    value_refs = refs[1 + views : 1 + 2 * views]
    spatial_ref, joined_ref = refs[1 + 2 * views :]
    head_width = LANES // 2
    source = (lax.broadcasted_iota(jnp.int32, (2 * LANES, LANES), 0) % LANES) // head_width
    target = lax.broadcasted_iota(jnp.int32, (2 * LANES, LANES), 1) // head_width
    spread = jnp.where(source == target, 1.0, 0.0).astype(jnp.bfloat16)
    for j in range(group):
        lanes = slice(j * LANES, (j + 1) * LANES)
        query = query_ref[0, 0, :, lanes].astype(jnp.float32)
        scores = []
        for key_ref in key_refs:
            product = query * key_ref[0, 0, 0, :, lanes].astype(jnp.float32)
            high = product.astype(jnp.bfloat16)
            low = (product - high.astype(jnp.float32)).astype(jnp.bfloat16)
            both = jnp.concatenate([high, low], axis=1)
            scores.append(
                jnp.dot(both, spread, preferred_element_type=jnp.float32)
                * (head_width ** (-0.5))
            )
        top = functools.reduce(jnp.maximum, scores)
        expo = [jnp.exp(score - top) for score in scores]
        inverse = 1.0 / functools.reduce(jnp.add, expo)
        joined = None
        for value_ref, part in zip(value_refs, expo):
            weight = (part * inverse).astype(jnp.bfloat16).astype(jnp.float32)
            term = weight * value_ref[0, j].astype(jnp.float32)
            joined = term if joined is None else joined + term
        joined_ref[0, 0, :, lanes] = joined.astype(joined_ref.dtype)
        spatial_ref[0, 0, :, lanes] = value_refs[0][0, j]


def combine(view, carry, view_queries, keys, outputs, first_batch):
    batch_size, single, rows, width = view_queries.shape
    parts = outputs[0].shape[-3]
    views = len(outputs)
    group = 4
    steps = width // LANES // group

    def place(i, view_ref):
        return (first_batch + i // steps, 0, 0, i % steps)

    def key_place(shift, i, view_ref):
        return (view_ref[0] ^ shift,) + place(i, view_ref)

    wide = pl.BlockSpec((1, 1, rows, group * LANES), place)
    key_specs = [
        pl.BlockSpec((1, 1, 1, rows, group * LANES), functools.partial(key_place, shift))
        for shift in range(views)
    ]

    def output_place(shift, i, view_ref):
        return (view_ref[0] ^ shift if outputs[shift].shape[0] > 1 else 0, i, 0, 0)

    output_specs = [
        pl.BlockSpec((1, group, rows, LANES), functools.partial(output_place, shift))
        for shift in range(views)
    ]
    shape = jax.ShapeDtypeStruct(view_queries.shape, view_queries.dtype)
    carried = len(carry)
    return pl.pallas_call(
        functools.partial(combine_kernel, views, group, carried),
        grid_spec=pltpu.PrefetchScalarGridSpec(
            num_scalar_prefetch=1,
            grid=(parts // group,),
            in_specs=[pl.BlockSpec(memory_space=pl.ANY)] * carried
            + [wide]
            + key_specs
            + output_specs,
            out_specs=[wide, wide],
        ),
        out_shape=[shape, shape],
        input_output_aliases={1 + i: i for i in range(carried)},
        cost_estimate=pl.CostEstimate(
            flops=parts * rows * LANES * 1024 * views,
            bytes_accessed=parts * rows * LANES * 2 * (2 * views + 3),
            transcendentals=parts * rows * LANES * (views + 1),
        ),
        name="combine",
    )(view, *carry, view_queries, *[keys] * views, *outputs)


def swap(blocks, axis, size, stride):
    arrived = list(blocks)
    for shift in reversed(range(1, len(blocks))):
        arrived[shift] = lax.ppermute(
            blocks[shift], axis, [(i, i ^ (shift * stride)) for i in range(size)]
        )
    return arrived


def local(seq_size, views, queries, key_rows, value_rows, view_queries):
    batch_size, single, rows, width = queries.shape
    per_chunk = seq_size // (width // LANES)
    chunks = batch_size // per_chunk
    near = split_size(seq_size)
    me = lax.axis_index("seq").astype(jnp.int32).reshape(1)
    view = lax.axis_index("view").astype(jnp.int32).reshape(1)
    exchange = functools.partial(
        lax.all_to_all, axis_name="seq", split_axis=0, concat_axis=0, tiled=True
    )
    neighbours = [list(range(i, i + near)) for i in range(0, seq_size, near)]
    keys = lax.all_gather(key_rows, "view")
    sources = (queries, key_rows, value_rows)
    packed, crossed, received = [], [], []
    for c in range(chunks):
        after = tuple(blocks[0] for blocks in packed[-1:])
        packed.append(pack(me, sources, c * per_chunk, per_chunk, seq_size, after))
        crossed.append(swap(packed[c], "seq", seq_size, near))
    repacked, received = [], []

    def arrive(c, after):
        repacked.append(repack(me, crossed[c], 2 * c < chunks, after))
        if 2 * c < chunks:
            received.append([exchange(repacked[c][0], axis_index_groups=neighbours)])
        else:
            received.append(swap(repacked[c], "seq", seq_size, 1))

    arrive(0, ())
    carry, attended = (), ()
    for c in range(chunks):
        after = attended + tuple(blocks[1] for blocks in crossed[c + 1 : c + 2])
        if c + 1 < chunks - 1:
            arrive(c + 1, attended or (repacked[0][0],))
            after += (repacked[c + 1][0],)
        if c == 1:
            after += (keys,)
        attended = (attend(me, received[c], seq_size, after),)
        if c + 1 == chunks - 1:
            arrive(c + 1, attended)
        returned = exchange(attended[0])
        own = returned[None]
        if c == 0 and chunks > 2:
            outputs = [own] + [lax.all_gather(returned, "view")] * (views - 1)
        else:
            outputs = swap([own] * views, "view", views, 1)
        carry = combine(view, carry, view_queries, keys, outputs, c * per_chunk)
    return tuple(carry)


def solution(mesh):
    spec = P(None, "view", "seq", None)
    return jax.shard_map(
        functools.partial(local, mesh.shape["seq"], mesh.shape["view"]),
        mesh=mesh,
        in_specs=(spec,) * 4,
        out_specs=(spec, spec),
        check_vma=False,
    )
```
